32 devices in a mesh: section: 2 (over x), dp: 16 (over z, y, core).
Axes of the slice: x: 2, y: 2, z: 4, core: 2. Of those that a mesh axis runs over, the one named last changes fastest.
Arguments:
- section_in: bfloat16 [2, 4, 16, 128, 1536], P('section', None, 'dp'), may hold values from -6 to 6
- top_grad: bfloat16 [4, 16, 128, 1536], P(None, 'dp'), may hold values from -0.029907227 to 0.029907227
- seq_lengths: int32 [4, 16], P(None, 'dp'), may hold values from 32 to 128, as said below
- lang_labels: int32 [4, 16], P(None, 'dp'), may hold values from 0 to 28
- norm_gain: float32 [2, 1536], P('section'), may hold values from 0.5 to 1.5
- w_down: bfloat16 [2, 1536, 256], P('section'), may hold values from -0.15625 to 0.15625
- w_up: bfloat16 [2, 256, 1536], P('section'), may hold values from -0.375 to 0.375
- critic_first: bfloat16 [1536, 768], P('section'), may hold values from -0.15625 to 0.15625
- critic_second: bfloat16 [768, 29], replicated, may hold values from -0.21875 to 0.21875
Outputs:
- grad_w_down: float32 [2, 1536, 256], P('section', 'dp')
- grad_w_up: float32 [2, 256, 1536], P('section', None, 'dp')
- grad_norm_gain: float32 [2, 1536], P('section', 'dp')
- grad_critic_first: float32 [1536, 768], P('section', 'dp')
- grad_critic_second: float32 [768, 29], P('dp')
The draws below stay inside these ranges and needn't reach their ends.
Inputs may be any that keep to these rules, and one draw needn't show every extreme that they name: `seq_lengths`: in every draw some sequence has all 128 tokens valid.
All inputs are finite; a program needn't handle non-finite values.
Results may differ from the reference program's by a relative error of at most 0.023.
Values may be sent and summed in bfloat16 or wider, within the bound.
A program may use at most 64 MiB of HBM per device.

```python
import jax
import jax.numpy as jnp
from jax import lax

D = 1536
R = 256
CH = 768
NLANG = 29
MICRO = 4
LEN = 128
NSEQ = 16
N_SECTION = 2


def draw_seq_lengths(key, part):
    first_key, second_key = jax.random.split(jax.random.fold_in(key, 11))
    drawn = jax.random.randint(first_key, (MICRO * NSEQ,), LEN // 4, LEN + 1)
    chosen = jax.random.randint(second_key, (), 0, MICRO * NSEQ)
    filled = jnp.where(jnp.arange(MICRO * NSEQ) == chosen, LEN, drawn)
    return filled.reshape(MICRO, NSEQ).astype(jnp.int32)


def set_ends(values, rng, smallest, largest):
    extent = values.shape
    index_at = [jax.random.randint(jax.random.fold_in(rng, axis), (), 0, extent[axis]) for axis in range(len(extent))]
    values = values.at[tuple(index_at)].set(smallest)
    longest = extent.index(max(extent))
    index_at[longest] = (index_at[longest] + 1) % extent[longest]
    return values.at[tuple(index_at)].set(largest)


def strengthened(values, rng, source, target, shards_of, factor):
    owner, partner = [(jnp.arange(values.shape[dim]) // (values.shape[dim] // shards_of)).reshape([-1 if axis == dim else 1 for axis in range(values.ndim)]) for dim in (source, target)]
    chosen = jax.random.permutation(rng, shards_of)[partner]
    strong = (owner == chosen) | (owner == (partner + shards_of // 2) % shards_of)
    return jnp.where(strong, factor * values, values)


def shard_levels(stream_key, dims, shards, least, top_value):
    def one(dim, blocks):
        draws = jax.random.uniform(jax.random.fold_in(jax.random.fold_in(stream_key, 6), dim), (blocks,), jnp.float32, least / len(shards), top_value / len(shards))
        return jnp.repeat(jnp.exp(draws), dims[dim] // blocks).reshape((-1,) + (1,) * (len(dims) - dim - 1))

    loudness = one(*shards[0])
    for cut in shards[1:]:
        loudness = loudness * one(*cut)
    return loudness


def noise(own_key, dims, scale, most, cuts=(), held_as=jnp.bfloat16):
    level = shard_levels(own_key, dims, cuts, -0.22, 0.18) if cuts else 1.0
    values = jax.random.normal(own_key, dims, jnp.float32) * scale * level
    return jnp.minimum(jnp.maximum(values, -most), most).astype(held_as)


def gaussian_with(own_key, extent, deviation, limit, pieces, heavy, dtype=jnp.bfloat16):
    result = deviation * jax.random.normal(own_key, extent, jnp.float32)
    if pieces:
        result = result * shard_levels(own_key, extent, pieces, -0.22, 0.18)
    return jnp.clip(strengthened(result, jax.random.fold_in(own_key, 3), *heavy), -limit, limit).astype(dtype)


def setup_inputs(seed: int = 0) -> dict:
    arg_keys = jax.random.split(jax.random.key(seed), 10)
    return {
        "section_in": noise(arg_keys[0], (N_SECTION, MICRO, NSEQ, LEN, D), 1.0, 6.0, ((0, 2), (2, 16))),
        "top_grad": gaussian_with(arg_keys[1], (MICRO, NSEQ, LEN, D), 0.005, 0.029907227, ((1, 16),), (1, 3, 16, 2.0)),
        "seq_lengths": draw_seq_lengths(jax.random.fold_in(arg_keys[9], 71), 0),
        "lang_labels": set_ends(jax.random.randint(arg_keys[3], (MICRO, NSEQ), 0, NLANG), jax.random.fold_in(arg_keys[3], 1), 0, NLANG - 1).astype(jnp.int32),
        "norm_gain": jnp.clip(1.0 + 0.1 * jax.random.normal(arg_keys[4], (N_SECTION, D), jnp.float32), 0.5, 1.5),
        "w_down": noise(arg_keys[5], (N_SECTION, D, R), D ** -0.5, 0.15625, ((0, 2),)),
        "w_up": noise(arg_keys[6], (N_SECTION, R, D), R ** -0.5, 0.375, ((0, 2),)),
        "critic_first": noise(arg_keys[7], (D, CH), D ** -0.5, 0.15625, ((0, 2),)),
        "critic_second": noise(arg_keys[8], (CH, NLANG), CH ** -0.5, 0.21875),
    }


EPSILON = 1e-06
REVERSAL = 0.5

def silu_slope(pre_act):
    sigma = jax.nn.sigmoid(pre_act)
    return sigma * (1.0 + pre_act * (1.0 - sigma))

def inner_rows(left, right):
    return lax.dot_general(left, right, (((0,), (0,)), ((), ())), preferred_element_type=jnp.float32)

def adapter_backward(local_rows, upstream, gain_row, down_proj, up_proj):
    values = local_rows.astype(jnp.float32)
    inv_rms = lax.rsqrt(lax.optimization_barrier(jnp.mean(values * values, axis=-1, keepdims=True)) + EPSILON)
    unit_rows = values * inv_rms
    normed = (unit_rows * gain_row[None, :]).astype(jnp.bfloat16)
    pre_act = jnp.dot(normed, down_proj, preferred_element_type=jnp.float32)
    hidden = jax.nn.silu(pre_act).astype(jnp.bfloat16)
    grad_up = inner_rows(hidden, upstream)
    grad_hidden = jnp.dot(upstream, up_proj.T, preferred_element_type=jnp.float32)
    grad_pre = (grad_hidden * silu_slope(pre_act)).astype(jnp.bfloat16)
    grad_down = inner_rows(normed, grad_pre)
    grad_normed = jnp.dot(grad_pre, down_proj.T, preferred_element_type=jnp.float32)
    grad_gain = lax.optimization_barrier(jnp.sum(grad_normed * unit_rows, axis=0))
    scaled = grad_normed * gain_row[None, :]
    grad_input = upstream.astype(jnp.float32) + inv_rms * (scaled - unit_rows * lax.optimization_barrier(jnp.mean(scaled * unit_rows, axis=-1, keepdims=True)))
    return (grad_input, grad_down, grad_up, grad_gain)

def reference(section_in, top_grad, seq_lengths, lang_labels, norm_gain, w_down, w_up, critic_first, critic_second):
    target = N_SECTION // 2
    positions = jnp.arange(LEN)
    valid_mask = (positions[None, None, :] < seq_lengths[:, :, None]).astype(jnp.float32)
    lengths = seq_lengths.astype(jnp.float32)
    totals = jnp.einsum('mnt,mntd->mnd', valid_mask, section_in[target].astype(jnp.float32))
    pooled = (totals / lengths[:, :, None]).astype(jnp.bfloat16)
    batch_rows = MICRO * NSEQ
    values = pooled.reshape(batch_rows, D).astype(jnp.float32)
    inv_rms = lax.rsqrt(lax.optimization_barrier(jnp.mean(values * values, axis=-1, keepdims=True)) + EPSILON)
    unit_rows = values * inv_rms
    normed = unit_rows.astype(jnp.bfloat16)
    pre_act = jnp.dot(normed, critic_first, preferred_element_type=jnp.float32)
    hidden = jax.nn.silu(pre_act).astype(jnp.bfloat16)
    logits = jnp.dot(hidden, critic_second, preferred_element_type=jnp.float32)
    exponent = jnp.exp(logits)
    probabilities = exponent / lax.optimization_barrier(jnp.sum(exponent, axis=-1, keepdims=True))
    onehot = (lang_labels.reshape(batch_rows)[:, None] == jnp.arange(NLANG)[None, :]).astype(jnp.float32)
    grad_logits = (probabilities - onehot).astype(jnp.bfloat16)
    grad_second = inner_rows(hidden, grad_logits)
    grad_hidden = jnp.dot(grad_logits, critic_second.T, preferred_element_type=jnp.float32)
    grad_pre = (grad_hidden * silu_slope(pre_act)).astype(jnp.bfloat16)
    grad_first = inner_rows(normed, grad_pre)
    grad_normed = jnp.dot(grad_pre, critic_first.T, preferred_element_type=jnp.float32)
    grad_pooled = inv_rms * (grad_normed - unit_rows * lax.optimization_barrier(jnp.mean(grad_normed * unit_rows, axis=-1, keepdims=True)))
    reversal = (-REVERSAL * grad_pooled / lengths.reshape(batch_rows)[:, None]).reshape(MICRO, NSEQ, D)
    down_sums = [jnp.zeros((D, R), jnp.float32) for level in range(N_SECTION)]
    up_sums = [jnp.zeros((R, D), jnp.float32) for level in range(N_SECTION)]
    gain_sums = [jnp.zeros((D,), jnp.float32) for level in range(N_SECTION)]
    for micro_index in range(MICRO):
        upstream = top_grad[micro_index].reshape(NSEQ * LEN, D)
        for level in reversed(range(N_SECTION)):
            local_rows = section_in[level, micro_index].reshape(NSEQ * LEN, D)
            grad_input, grad_down, grad_up, grad_gain = adapter_backward(local_rows, upstream, norm_gain[level], w_down[level], w_up[level])
            down_sums[level] = down_sums[level] + grad_down
            up_sums[level] = up_sums[level] + grad_up
            gain_sums[level] = gain_sums[level] + grad_gain
            if level == target:
                extra = reversal[micro_index][:, None, :] * valid_mask[micro_index][:, :, None]
                grad_input = grad_input + extra.reshape(NSEQ * LEN, D)
            upstream = grad_input.astype(jnp.bfloat16)
    return (jnp.stack(down_sums), jnp.stack(up_sums), jnp.stack(gain_sums), grad_first, grad_second)
```

```python
import functools

import jax
import jax.numpy as jnp
from jax import lax
from jax.experimental import pallas as pl
from jax.experimental.pallas import tpu as pltpu
from jax.sharding import PartitionSpec as P

EPSILON = 1e-06
REVERSAL = 0.5
PAD = 16
LANES = 128
F32 = jnp.float32
BF16 = jnp.bfloat16
MESH = pl.DeviceIdType.MESH


def contract(left, right, left_dim, right_dim):
    return lax.dot_general(
        left, right, (((left_dim,), (right_dim,)), ((), ())), preferred_element_type=F32
    )


def bit_orders(bits):
    near = list(range(bits))
    return near, ([0] + near[2:] + [1] if bits > 1 else near)


def relay_kernel(
    sizes,
    lengths_ref,
    labels_ref,
    x_ref,
    g_ref,
    gain_ref,
    gain_cut_ref,
    wd_ref,
    wu_ref,
    cf_ref,
    cs_ref,
    gwd_ref,
    gwu_ref,
    gain_out_ref,
    first_ref,
    second_ref,
    *scratch,
):
    micro, length, bits, chunk = sizes
    (
        xn_ref,
        g0_ref,
        h_ref,
        da_ref,
        slope_ref,
        wu_in_ref,
        h0_ref,
        p_ref,
        p_in_ref,
        pool_ref,
        pre_ref,
        pre_in_ref,
        gn_ref,
        gn_in_ref,
        cs_pad_ref,
        pack32_ref,
        ag_ref,
        last_ref,
        last_in_ref,
        *job_refs,
        x_sems,
        ag_sems,
        rs_sems,
    ) = scratch
    dp = 1 << bits
    tokens, features = x_ref.shape
    rank = wd_ref.shape[1]
    band, hidden_width = cf_ref.shape
    languages = cs_ref.shape[1]
    cut = features // dp
    section = lax.axis_index("section")
    replica = lax.axis_index("dp")
    across = (1 - section, replica)

    def peer(bit):
        mine = lax.rem(replica // (1 << bit), 2)
        return mine, (section, replica + (1 - 2 * mine) * (1 << bit))

    orders = bit_orders(bits)
    job_order = (orders[0], orders[1], orders[0])
    cuts = [job_refs[job * 2 * bits : job * 2 * bits + bits] for job in range(3)]
    lands = [job_refs[job * 2 * bits + bits : (job + 1) * 2 * bits] for job in range(3)]

    def x_copy(slot, src, dst, device):
        return pltpu.make_async_remote_copy(
            src_ref=src,
            dst_ref=dst,
            send_sem=x_sems.at[2 * slot],
            recv_sem=x_sems.at[2 * slot + 1],
            device_id=device,
            device_id_type=MESH,
        )

    core, beside = peer(0)
    half_rank = rank // 2
    my_half = wu_ref.at[pl.ds(pl.multiple_of(core * half_rank, half_rank), half_rank)]
    my_half_in = wu_in_ref.at[pl.ds(pl.multiple_of(core * half_rank, half_rank), half_rank)]
    up_across = x_copy(0, my_half, my_half_in, across)
    up_beside = x_copy(1, my_half_in, my_half_in, beside)
    pool_across = x_copy(2, pool_ref, pool_ref, across)
    pre_across = x_copy(3, pre_ref, pre_in_ref, across)
    gn_across = x_copy(4, gn_ref, gn_in_ref, across)
    h_across = x_copy(5, h_ref, h0_ref, across)
    p_across = x_copy(6, p_ref, p_in_ref, across)
    last_across = x_copy(7, last_ref, last_in_ref, across)

    def ag_copy(step):
        count = 1 << step
        return pltpu.make_async_remote_copy(
            src_ref=ag_ref.at[pl.ds(0, count)],
            dst_ref=ag_ref.at[pl.ds(count, count)],
            send_sem=ag_sems.at[2 * step],
            recv_sem=ag_sems.at[2 * step + 1],
            device_id=peer(bits - 1 - step)[1],
            device_id_type=MESH,
        )

    def rs_copy(job, step):
        count = dp >> (step + 1)
        mine, other = peer(job_order[job][step])
        return pltpu.make_async_remote_copy(
            src_ref=cuts[job][step].at[pl.ds((1 - mine) * count, count)],
            dst_ref=lands[job][step],
            send_sem=rs_sems.at[2 * (job * bits + step)],
            recv_sem=rs_sems.at[2 * (job * bits + step) + 1],
            device_id=other,
            device_id_type=MESH,
        )

    def rs_take(job, step):
        count = dp >> (step + 1)
        mine = peer(job_order[job][step])[0]
        rs_copy(job, step).wait_recv()
        kept = cuts[job][step][pl.ds(mine * count, count)].astype(F32)
        return kept + lands[job][step][...].astype(F32)

    def rs_step(job, step):
        cuts[job][step + 1][...] = rs_take(job, step).astype(BF16)
        rs_copy(job, step + 1).start()

    def fill(job, left_ref, right_ref, extra=None):
        group = 4 * cut
        for part in range(features // group):
            columns = pl.ds(part * group, group)
            product = contract(left_ref[:, columns], right_ref[...], 0, 0)
            if extra is not None:
                product += contract(
                    extra[0][:, part * group : (part + 1) * group], extra[1], 0, 0
                )
            product = product.astype(BF16)
            for inner in range(4):
                target = part * 4 + inner
                place = 0
                for step, bit in enumerate(job_order[job]):
                    place += ((target >> bit) & 1) << (bits - 1 - step)
                cuts[job][0][place] = product[inner * cut : (inner + 1) * cut]

    barrier = pltpu.get_barrier_semaphore()
    pl.semaphore_signal(barrier, inc=1, device_id=across, device_id_type=MESH)
    for bit in range(bits):
        pl.semaphore_signal(barrier, inc=1, device_id=peer(bit)[1], device_id_type=MESH)
    pl.semaphore_wait(barrier, bits + 1)

    row_of = lax.broadcasted_iota(jnp.int32, (PAD, tokens), 0)
    token_of = lax.broadcasted_iota(jnp.int32, (PAD, tokens), 1)
    valid = jnp.zeros((PAD, tokens), F32)
    pad_rows = lax.broadcasted_iota(jnp.int32, (PAD, 1), 0)
    lengths = jnp.ones((PAD, 1), F32)
    labels = jnp.full((PAD, 1), -1, jnp.int32)
    for m in range(micro):
        seq = lengths_ref[m, 0]
        inside = (row_of == m) & (token_of >= m * length) & (token_of < m * length + seq)
        valid = jnp.where(inside, 1.0, valid)
        lengths = jnp.where(pad_rows == m, seq.astype(F32), lengths)
        labels = jnp.where(pad_rows == m, labels_ref[m, 0], labels)
    valid = valid.astype(BF16)

    def normalised(rows):
        values = x_ref[rows, :].astype(F32)
        inv_rms = lax.rsqrt(jnp.mean(values * values, axis=-1, keepdims=True) + EPSILON)
        unit = values * inv_rms
        xn = (unit * gain_ref[...]).astype(BF16)
        xn_ref[rows, :] = xn
        pre_act = contract(xn, wd_ref[...], 1, 0)
        sigma = jax.nn.sigmoid(pre_act)
        h_ref[rows, :] = (pre_act * sigma).astype(BF16)
        return inv_rms, unit, sigma * (1.0 + pre_act * (1.0 - sigma))

    @pl.when(section == 0)
    def _():
        up_across.start()

        @pl.loop(0, tokens // chunk)
        def _(index):
            rows = pl.ds(pl.multiple_of(index * chunk, chunk), chunk)
            slope_ref[rows, :] = normalised(rows)[2]

        h_across.start()
        pool_across.wait_recv()

    @pl.when(section == 1)
    def _():
        totals = contract(valid, x_ref[...], 1, 0)
        pool_ref[...] = (totals / lengths).astype(BF16)
        pool_across.start()

    pooled = pool_ref[...].astype(F32)
    pooled_inv = lax.rsqrt(jnp.mean(pooled * pooled, axis=-1, keepdims=True) + EPSILON)
    pooled_unit = pooled * pooled_inv
    pooled_normed = jnp.where(section == 0, pooled_unit[:, :band], pooled_unit[:, band:])
    pre_ref[...] = contract(pooled_normed.astype(BF16), cf_ref[...], 1, 0)
    pre_across.start()
    cs_pad_ref[...] = jnp.zeros(cs_pad_ref.shape, BF16)
    cs_pad_ref[:, :languages] = cs_ref[...]

    @pl.when(section == 1)
    def _():
        @pl.loop(0, tokens // chunk)
        def _(index):
            rows = pl.ds(pl.multiple_of(index * chunk, chunk), chunk)
            inv_rms, unit, slope = normalised(rows)
            upstream = g_ref[rows, :]
            grad_hidden = contract(upstream, wu_ref[...], 1, 1)
            da = (grad_hidden * slope).astype(BF16)
            da_ref[rows, :] = da
            scaled = contract(da, wd_ref[...], 1, 1) * gain_ref[...]
            tilt = jnp.mean(scaled * unit, axis=-1, keepdims=True)
            g0_ref[rows, :] = (
                upstream.astype(F32) + inv_rms * (scaled - unit * tilt)
            ).astype(BF16)

        fill(0, xn_ref, da_ref)
        rs_copy(0, 0).start()
        fill(1, g_ref, h_ref)
        rs_copy(1, 0).start()
        up_across.wait_recv()
        up_beside.start()

    pre_across.wait_recv()
    pre = pre_ref[...] + pre_in_ref[...]
    sigma = jax.nn.sigmoid(pre)
    hidden = (pre * sigma).astype(BF16)
    logits = contract(hidden, cs_pad_ref[...], 1, 0)
    language = lax.broadcasted_iota(jnp.int32, (PAD, LANES), 1)
    exponent = jnp.where(language < languages, jnp.exp(logits), 0.0)
    probabilities = exponent / jnp.sum(exponent, axis=-1, keepdims=True)
    onehot = jnp.where(language == labels, 1.0, 0.0)
    grad_logits = (probabilities - onehot).astype(BF16)
    grad_hidden = contract(grad_logits, cs_pad_ref[...], 1, 1)
    grad_pre = (grad_hidden * (sigma * (1.0 + pre * (1.0 - sigma)))).astype(BF16)
    gn_ref[...] = contract(grad_pre, cf_ref[...], 1, 1)

    @pl.when(section == 0)
    def _():
        gn_across.start()

    pack32_ref[...] = jnp.zeros(pack32_ref.shape, F32)
    pack32_ref[0:micro, :band] = pooled_normed[:micro]
    pack32_ref[micro : 2 * micro, :hidden_width] = hidden.astype(F32)[:micro]
    pack32_ref[2 * micro : 3 * micro, :hidden_width] = grad_pre.astype(F32)[:micro]
    pack32_ref[3 * micro : 4 * micro, :LANES] = grad_logits.astype(F32)[:micro]
    ag_ref[0] = pack32_ref[...].astype(BF16)
    ag_copy(0).start()

    @pl.when(section == 1)
    def _():
        gn_across.wait_recv()
        grad_normed = jnp.concatenate([gn_in_ref[...], gn_ref[...]], axis=1)
        tilt = jnp.mean(grad_normed * pooled_unit, axis=-1, keepdims=True)
        grad_pooled = pooled_inv * (grad_normed - pooled_unit * tilt)
        in_use = pad_rows < micro
        reversal = jnp.where(in_use, -REVERSAL * grad_pooled / lengths, 0.0).astype(BF16)
        up_beside.wait_recv()
        up_reversal = contract(reversal, wu_in_ref[...], 1, 1)
        for m in range(micro):
            rows = pl.ds(m * length, length)
            inside = lax.broadcasted_iota(jnp.int32, (length, 1), 0) < lengths_ref[m, 0]
            extra = jnp.where(inside, up_reversal[m : m + 1], 0.0)
            p_ref[rows, :] = (contract(g0_ref[rows, :], wu_in_ref[...], 1, 1) + extra).astype(BF16)
        p_across.start()
        rs_step(0, 0)
        rs_step(1, 0)
        h_across.wait_recv()
        masked_h = contract(valid, h0_ref[...], 1, 0).astype(BF16)
        fill(2, g0_ref, h0_ref, (reversal, masked_h))
        rs_copy(2, 0).start()

    def ag_step(step):
        ag_copy(step).wait_recv()
        if step + 1 < bits:
            ag_copy(step + 1).start()

    def critic_outputs():
        blocks = ag_ref[...].reshape(dp * PAD, ag_ref.shape[2])
        total = dp * PAD
        from_row = lax.broadcasted_iota(jnp.int32, (total, total), 1)
        to_row = lax.broadcasted_iota(jnp.int32, (total, total), 0)
        early = lax.rem(to_row, PAD) < 2 * micro
        shift = jnp.where(early & (from_row == to_row + 2 * micro), 1.0, 0.0).astype(BF16)
        own = hidden_width // dp
        at = lax.broadcasted_iota(jnp.int32, (blocks.shape[1], LANES), 0)
        lane = lax.broadcasted_iota(jnp.int32, (blocks.shape[1], LANES), 1)
        pick = jnp.where((at == lane + replica * own) & (lane < own), 1.0, 0.0).astype(BF16)
        picked = contract(blocks, pick, 1, 0)
        place = lax.rem(lax.broadcasted_iota(jnp.int32, (total, LANES), 0), PAD)
        moved_pre = contract(shift, picked.astype(BF16), 1, 0)
        moved_pre = jnp.where(place < micro, moved_pre, 0.0).astype(BF16)
        moved_logits = contract(shift, blocks[:, :LANES], 1, 0).astype(BF16)
        hidden_own = jnp.where((place >= micro) & (place < 2 * micro), picked, 0.0).astype(BF16)
        first_ref[...] = contract(blocks[:, :band], moved_pre, 0, 0)[:, :own]
        second_ref[...] = contract(hidden_own, moved_logits, 0, 0)[:own, :languages]

    def finish_down():
        reduced = rs_take(0, bits - 1)[0]
        gwd_ref[...] = reduced
        start = pl.multiple_of(replica * cut, cut)
        weighted = reduced * wd_ref[pl.ds(start, cut), :].astype(F32)
        row = lax.dot_general(
            jnp.ones((8, rank), F32),
            weighted,
            (((1,), (1,)), ((), ())),
            precision=lax.Precision.HIGHEST,
            preferred_element_type=F32,
        )
        gain_out_ref[...] = row[0:1] / gain_cut_ref[pl.ds(replica, 1), :]

    @pl.when(section == 1)
    def _():
        for step in range(bits):
            ag_step(step)
            if step + 1 < bits:
                rs_step(2, step)
            if step + 2 < bits:
                rs_step(0, step + 1)
                rs_step(1, step + 1)
        last_ref[...] = rs_take(2, bits - 1)[0]
        last_across.start()
        finish_down()
        gwu_ref[...] = rs_take(1, bits - 1)[0]
        critic_outputs()

    @pl.when(section == 0)
    def _():
        for step in range(bits):
            ag_step(step)
        critic_outputs()
        p_across.wait_recv()
        da_ref[...] = (p_in_ref[...].astype(F32) * slope_ref[...]).astype(BF16)
        fill(0, xn_ref, da_ref)
        rs_copy(0, 0).start()
        for step in range(bits - 1):
            rs_step(0, step)
        finish_down()
        last_across.wait_recv()
        gwu_ref[...] = last_in_ref[...]

    pre_across.wait_send()
    for step in range(bits):
        ag_copy(step).wait_send()
        rs_copy(0, step).wait_send()

    @pl.when(section == 0)
    def _():
        up_across.wait_send()
        h_across.wait_send()
        gn_across.wait_send()

    @pl.when(section == 1)
    def _():
        up_beside.wait_send()
        pool_across.wait_send()
        p_across.wait_send()
        last_across.wait_send()
        for step in range(bits):
            rs_copy(1, step).wait_send()
            rs_copy(2, step).wait_send()


def fused_body(
    section_in,
    top_grad,
    seq_lengths,
    lang_labels,
    norm_gain,
    w_down,
    w_up,
    critic_first,
    critic_second,
):
    dp = lax.axis_size("dp")
    bits = dp.bit_length() - 1
    micro, _, length, features = section_in.shape[1:]
    tokens = micro * length
    rank = w_down.shape[2]
    band, hidden_width = critic_first.shape
    languages = critic_second.shape[1]
    cut = features // dp
    width = max(band, hidden_width)
    chunk = min(2 * length, tokens)
    jobs = []
    for _ in range(3):
        jobs += [pltpu.VMEM((dp >> step, cut, rank), BF16) for step in range(bits)]
        jobs += [pltpu.VMEM((dp >> (step + 1), cut, rank), BF16) for step in range(bits)]
    vmem = pl.BlockSpec(memory_space=pltpu.VMEM)
    smem = pl.BlockSpec(memory_space=pltpu.SMEM)
    gwd, gwu, gain, first, second = pl.pallas_call(
        functools.partial(relay_kernel, (micro, length, bits, chunk)),
        out_shape=(
            jax.ShapeDtypeStruct((cut, rank), F32),
            jax.ShapeDtypeStruct((cut, rank), F32),
            jax.ShapeDtypeStruct((1, cut), F32),
            jax.ShapeDtypeStruct((band, hidden_width // dp), F32),
            jax.ShapeDtypeStruct((hidden_width // dp, languages), F32),
        ),
        in_specs=[smem, smem] + [vmem] * 8,
        out_specs=(vmem,) * 5,
        scratch_shapes=[
            pltpu.VMEM((tokens, features), BF16),
            pltpu.VMEM((tokens, features), BF16),
            pltpu.VMEM((tokens, rank), BF16),
            pltpu.VMEM((tokens, rank), BF16),
            pltpu.VMEM((tokens, rank), F32),
            pltpu.VMEM((rank, features), BF16),
            pltpu.VMEM((tokens, rank), BF16),
            pltpu.VMEM((tokens, rank), BF16),
            pltpu.VMEM((tokens, rank), BF16),
            pltpu.VMEM((PAD, features), BF16),
            pltpu.VMEM((PAD, hidden_width), F32),
            pltpu.VMEM((PAD, hidden_width), F32),
            pltpu.VMEM((PAD, band), F32),
            pltpu.VMEM((PAD, band), F32),
            pltpu.VMEM((hidden_width, LANES), BF16),
            pltpu.VMEM((PAD, width), F32),
            pltpu.VMEM((dp, PAD, width), BF16),
            pltpu.VMEM((cut, rank), F32),
            pltpu.VMEM((cut, rank), F32),
            *jobs,
            pltpu.SemaphoreType.DMA((16,)),
            pltpu.SemaphoreType.DMA((2 * bits,)),
            pltpu.SemaphoreType.DMA((6 * bits,)),
        ],
        compiler_params=pltpu.CompilerParams(
            collective_id=0, has_side_effects=True, vmem_limit_bytes=52 * 2**20
        ),
        cost_estimate=pl.CostEstimate(
            flops=12 * tokens * features * rank, bytes_accessed=8 * 2**20, transcendentals=0
        ),
    )(
        seq_lengths,
        lang_labels,
        section_in.reshape(tokens, features),
        top_grad.reshape(tokens, features),
        norm_gain,
        norm_gain.reshape(dp, cut),
        w_down[0],
        w_up[0],
        critic_first,
        critic_second,
    )
    return (gwd[None], gwu.T[None], gain, first, second)


def from_root(array, axis, root):
    mine = lax.axis_index(axis) == root
    return lax.psum(jnp.where(mine, array, jnp.zeros_like(array)), axis)


def from_behind(block, axis, distance):
    devices = range(lax.axis_size(axis))
    route = [(i - distance, i) for i in devices if i - distance in devices]
    return lax.ppermute(block, axis, route)


def silu_slope(pre_act):
    sigma = jax.nn.sigmoid(pre_act)
    return sigma * (1.0 + pre_act * (1.0 - sigma))


def inner_rows(left, right):
    return lax.dot_general(
        left, right, (((0,), (0,)), ((), ())), preferred_element_type=jnp.float32
    )


def adapter_backward(local_rows, upstream, gain_row, down_proj, up_proj):
    values = local_rows.astype(jnp.float32)
    inv_rms = lax.rsqrt(jnp.mean(values * values, axis=-1, keepdims=True) + EPSILON)
    unit_rows = values * inv_rms
    normed = (unit_rows * gain_row[None, :]).astype(jnp.bfloat16)
    pre_act = jnp.dot(normed, down_proj, preferred_element_type=jnp.float32)
    hidden = jax.nn.silu(pre_act).astype(jnp.bfloat16)
    grad_up = inner_rows(hidden, upstream)
    grad_hidden = jnp.dot(upstream, up_proj.T, preferred_element_type=jnp.float32)
    grad_pre = (grad_hidden * silu_slope(pre_act)).astype(jnp.bfloat16)
    grad_down = inner_rows(normed, grad_pre)
    grad_normed = jnp.dot(grad_pre, down_proj.T, preferred_element_type=jnp.float32)
    grad_gain = jnp.sum(grad_normed * unit_rows, axis=0)
    scaled = grad_normed * gain_row[None, :]
    grad_input = upstream.astype(jnp.float32) + inv_rms * (
        scaled - unit_rows * jnp.mean(scaled * unit_rows, axis=-1, keepdims=True)
    )
    return (grad_input, grad_down, grad_up, grad_gain)


def critic_pass(pooled, lang_labels, critic_first, critic_second, section_place):
    batch_rows = pooled.shape[0] * pooled.shape[1]
    features = pooled.shape[2]
    values = pooled.reshape(batch_rows, features).astype(jnp.float32)
    inv_rms = lax.rsqrt(jnp.mean(values * values, axis=-1, keepdims=True) + EPSILON)
    unit_rows = values * inv_rms
    normed = unit_rows.astype(jnp.bfloat16)
    band_rows = critic_first.shape[0]
    normed_band = lax.dynamic_slice_in_dim(normed, section_place * band_rows, band_rows, 1)
    full_first = lax.all_gather(critic_first, "section", axis=0, tiled=True)
    pre_act = jnp.dot(normed, full_first, preferred_element_type=jnp.float32)
    hidden = jax.nn.silu(pre_act).astype(jnp.bfloat16)
    logits = jnp.dot(hidden, critic_second, preferred_element_type=jnp.float32)
    exponent = jnp.exp(logits)
    probabilities = exponent / jnp.sum(exponent, axis=-1, keepdims=True)
    onehot = (
        lang_labels.reshape(batch_rows)[:, None] == jnp.arange(critic_second.shape[1])[None, :]
    ).astype(jnp.float32)
    grad_logits = (probabilities - onehot).astype(jnp.bfloat16)
    grad_second = inner_rows(hidden, grad_logits)
    grad_hidden = jnp.dot(grad_logits, critic_second.T, preferred_element_type=jnp.float32)
    grad_pre = (grad_hidden * silu_slope(pre_act)).astype(jnp.bfloat16)
    grad_first = inner_rows(normed_band, grad_pre)
    grad_normed = jnp.dot(grad_pre, full_first.T, preferred_element_type=jnp.float32)
    grad_pooled = inv_rms * (
        grad_normed - unit_rows * jnp.mean(grad_normed * unit_rows, axis=-1, keepdims=True)
    )
    return (grad_first, grad_second, grad_pooled)


def body(
    section_in,
    top_grad,
    seq_lengths,
    lang_labels,
    norm_gain,
    w_down,
    w_up,
    critic_first,
    critic_second,
):
    sections = lax.axis_size("section")
    section_place = lax.axis_index("section")
    target = sections // 2
    inputs = section_in[0]
    gain_row = norm_gain[0]
    down_proj = w_down[0]
    up_proj = w_up[0]
    micro_count, seq_dev, seq_len, features = inputs.shape
    token_rows = seq_dev * seq_len
    positions = jnp.arange(seq_len)
    valid_mask = positions[None, None, :] < seq_lengths[:, :, None]
    mask_values = valid_mask.astype(jnp.float32)
    lengths = seq_lengths.astype(jnp.float32)
    totals = jnp.einsum(
        "mnt,mntd->mnd", valid_mask.astype(jnp.bfloat16), inputs, preferred_element_type=jnp.float32
    )
    pooled = (totals / lengths[:, :, None]).astype(jnp.bfloat16)
    pooled = from_root(pooled, "section", target)
    grad_first, grad_second, grad_pooled = critic_pass(
        pooled, lang_labels, critic_first, critic_second, section_place
    )
    is_target = (section_place == target).astype(jnp.float32)
    reversal = (
        -REVERSAL
        * is_target
        * grad_pooled.reshape(micro_count, seq_dev, features)
        / lengths[:, :, None]
    )
    is_last = section_place == sections - 1

    def advance(moment, carry):
        incoming, down_sum, up_sum, gain_sum = carry
        micro_now = moment - (sections - 1 - section_place)
        is_live = (micro_now >= 0) & (micro_now < micro_count)
        slot_index = jnp.clip(micro_now, 0, micro_count - 1)
        local_rows = lax.dynamic_index_in_dim(inputs, slot_index, 0, keepdims=False).reshape(
            token_rows, features
        )
        top_rows = lax.dynamic_index_in_dim(top_grad, slot_index, 0, keepdims=False).reshape(
            token_rows, features
        )
        upstream = jnp.where(is_last, top_rows, incoming)
        reverse_rows = lax.dynamic_index_in_dim(reversal, slot_index, 0, keepdims=False)
        mask_rows = lax.dynamic_index_in_dim(mask_values, slot_index, 0, keepdims=False)
        extra = (reverse_rows[:, None, :] * mask_rows[:, :, None]).reshape(token_rows, features)

        def active(operand):
            grad_input, grad_down, grad_up, grad_gain = adapter_backward(
                local_rows, upstream, gain_row, down_proj, up_proj
            )
            return ((grad_input + extra).astype(jnp.bfloat16), grad_down, grad_up, grad_gain)

        def resting(operand):
            return (
                jnp.zeros_like(incoming),
                jnp.zeros_like(down_sum),
                jnp.zeros_like(up_sum),
                jnp.zeros_like(gain_sum),
            )

        outgoing, grad_down, grad_up, grad_gain = lax.cond(is_live, active, resting, 0)
        received = from_behind(outgoing, "section", -1)
        return (received, down_sum + grad_down, up_sum + grad_up, gain_sum + grad_gain)

    initial = (
        jnp.zeros((token_rows, features), jnp.bfloat16),
        jnp.zeros(down_proj.shape, jnp.float32),
        jnp.zeros(up_proj.shape, jnp.float32),
        jnp.zeros((features,), jnp.float32),
    )
    finished = lax.fori_loop(0, micro_count + sections - 1, advance, initial)
    summed = (
        lax.psum_scatter(finished[1], "dp", scatter_dimension=0, tiled=True),
        lax.psum_scatter(finished[2], "dp", scatter_dimension=1, tiled=True),
        lax.psum_scatter(finished[3], "dp", scatter_dimension=0, tiled=True),
        lax.psum_scatter(grad_first, "dp", scatter_dimension=1, tiled=True),
        lax.psum_scatter(grad_second, "dp", scatter_dimension=0, tiled=True),
    )
    return (summed[0][None], summed[1][None], summed[2][None], summed[3], summed[4])


def solution(mesh):
    sections, replicas = mesh.shape["section"], mesh.shape["dp"]

    def program(*args):
        micro, sequences = args[2].shape
        fits = (
            sections == 2
            and sequences == replicas
            and replicas >= 4
            and replicas & (replicas - 1) == 0
            and micro * 4 == PAD
            and args[4].shape[1] % (replicas * PAD) == 0
        )
        return placed(mesh, fused_body if fits else body)(*args)

    return program


def placed(mesh, device_body):
    return jax.shard_map(
        device_body,
        mesh=mesh,
        in_specs=(
            P("section", None, "dp", None, None),
            P(None, "dp", None, None),
            P(None, "dp"),
            P(None, "dp"),
            P("section", None),
            P("section", None, None),
            P("section", None, None),
            P("section", None),
            P(),
        ),
        out_specs=(
            P("section", "dp", None),
            P("section", None, "dp"),
            P("section", "dp"),
            P("section", "dp"),
            P("dp", None),
        ),
        check_vma=False,
    )
```

```python
import functools

import jax
import jax.numpy as jnp
from jax import lax
from jax.experimental import pallas as pl
from jax.experimental.pallas import tpu as pltpu
from jax.sharding import PartitionSpec as P

EPSILON = 1e-06
REVERSAL = 0.5
PAD = 16
LANES = 128
F32 = jnp.float32
BF16 = jnp.bfloat16
MESH = pl.DeviceIdType.MESH


def contract(left, right, left_dim, right_dim):
    return lax.dot_general(
        left, right, (((left_dim,), (right_dim,)), ((), ())), preferred_element_type=F32
    )


def bit_orders(bits):
    near = list(range(bits))
    return near, [0] + near[2:] + [1]


def relay_kernel(
    sizes,
    lengths_ref,
    labels_ref,
    x_hbm,
    g_hbm,
    gain_hbm,
    wd_hbm,
    wu_hbm,
    cf_hbm,
    cs_ref,
    gwd_ref,
    gwu_ref,
    gain_out_ref,
    first_ref,
    second_ref,
    *scratch,
):
    micro, length, bits, chunk = sizes
    (
        x_ref,
        g_ref,
        gain_ref,
        wd_ref,
        wu_ref,
        cf_ref,
        gain_cut_ref,
        xn_ref,
        g0_ref,
        h_ref,
        da_ref,
        slope_ref,
        wu_in_ref,
        h0_ref,
        p_ref,
        p_in_ref,
        pool_ref,
        pre_ref,
        pre_in_ref,
        gn_ref,
        gn_in_ref,
        cs_pad_ref,
        pack32_ref,
        ag_ref,
        last_ref,
        last_in_ref,
        *job_refs,
        load_sems,
        x_sems,
        p_sems,
        ag_sems,
        rs_sems,
    ) = scratch
    dp = 1 << bits
    tokens, features = x_ref.shape
    rank = wd_ref.shape[1]
    band, hidden_width = cf_ref.shape
    languages = cs_ref.shape[0]
    cut = features // dp
    section = lax.axis_index("section")
    replica = lax.axis_index("dp")
    across = (1 - section, replica)

    def peer(bit):
        mine = lax.rem(replica // (1 << bit), 2)
        return mine, (section, replica + (1 - 2 * mine) * (1 << bit))

    job_order = bit_orders(bits) * 3
    cuts = [job_refs[job * 2 * bits : job * 2 * bits + bits] for job in range(6)]
    lands = [job_refs[job * 2 * bits + bits : (job + 1) * 2 * bits] for job in range(6)]
    loads = [
        pltpu.make_async_copy(src, dst, load_sems.at[slot])
        for slot, (src, dst) in enumerate(
            (
                (x_hbm, x_ref),
                (wd_hbm, wd_ref),
                (gain_hbm, gain_ref),
                (cf_hbm, cf_ref),
                (g_hbm, g_ref),
                (wu_hbm, wu_ref),
            )
        )
    ]
    for load in loads[:4]:
        load.start()

    @pl.when(section == 1)
    def _():
        loads[4].start()
        loads[5].start()

    def x_copy(slot, src, dst, device):
        return pltpu.make_async_remote_copy(
            src_ref=src,
            dst_ref=dst,
            send_sem=x_sems.at[2 * slot],
            recv_sem=x_sems.at[2 * slot + 1],
            device_id=device,
            device_id_type=MESH,
        )

    core, beside = peer(0)
    half_rank = rank // 2
    my_half = wu_hbm.at[pl.ds(pl.multiple_of(core * half_rank, half_rank), half_rank)]
    my_half_in = wu_in_ref.at[pl.ds(pl.multiple_of(core * half_rank, half_rank), half_rank)]
    up_across = x_copy(0, my_half, my_half_in, across)
    up_beside = x_copy(1, my_half_in, my_half_in, beside)
    pool_across = x_copy(2, pool_ref, pool_ref, across)
    pre_across = x_copy(3, pre_ref, pre_in_ref, across)
    gn_across = x_copy(4, gn_ref, gn_in_ref, across)
    h_across = x_copy(5, h_ref, h0_ref, across)
    last_across = [
        x_copy(6 + side, last_ref.at[side], last_in_ref.at[side], across) for side in range(2)
    ]

    def p_copy(m):
        rows = pl.ds(m * length, length)
        return pltpu.make_async_remote_copy(
            src_ref=p_ref.at[rows],
            dst_ref=p_in_ref.at[rows],
            send_sem=p_sems.at[2 * m],
            recv_sem=p_sems.at[2 * m + 1],
            device_id=across,
            device_id_type=MESH,
        )

    def ag_copy(step):
        count = 1 << step
        return pltpu.make_async_remote_copy(
            src_ref=ag_ref.at[pl.ds(0, count)],
            dst_ref=ag_ref.at[pl.ds(count, count)],
            send_sem=ag_sems.at[2 * step],
            recv_sem=ag_sems.at[2 * step + 1],
            device_id=peer(bits - 1 - step)[1],
            device_id_type=MESH,
        )

    def rs_copy(job, step):
        count = dp >> (step + 1)
        mine, other = peer(job_order[job][step])
        return pltpu.make_async_remote_copy(
            src_ref=cuts[job][step].at[pl.ds((1 - mine) * count, count)],
            dst_ref=lands[job][step],
            send_sem=rs_sems.at[2 * (job * bits + step)],
            recv_sem=rs_sems.at[2 * (job * bits + step) + 1],
            device_id=other,
            device_id_type=MESH,
        )

    def rs_take(job, step):
        count = dp >> (step + 1)
        mine = peer(job_order[job][step])[0]
        rs_copy(job, step).wait_recv()
        kept = cuts[job][step][pl.ds(mine * count, count)].astype(F32)
        return kept + lands[job][step][...].astype(F32)

    def rs_step(job, step):
        cuts[job][step + 1][...] = rs_take(job, step).astype(BF16)
        rs_copy(job, step + 1).start()

    def fill(matrix, left_ref, right_ref, extra=None):
        group = 4 * cut
        for part in range(features // group):
            columns = pl.ds(part * group, group)
            product = contract(left_ref[:, columns], right_ref[...], 0, 0)
            if extra is not None:
                product += contract(
                    extra[0][:, part * group : (part + 1) * group], extra[1], 0, 0
                )
            product = product.astype(BF16)
            for inner in range(4):
                target = part * 4 + inner
                for side in range(2):
                    job = 2 * matrix + side
                    place = 0
                    for step, bit in enumerate(job_order[job]):
                        place += ((target >> bit) & 1) << (bits - 1 - step)
                    cuts[job][0][place] = product[
                        inner * cut : (inner + 1) * cut,
                        side * half_rank : (side + 1) * half_rank,
                    ]
        for side in range(2):
            rs_copy(2 * matrix + side, 0).start()

    def advance(matrix, step):
        rs_step(2 * matrix, step)
        rs_step(2 * matrix + 1, step)

    barrier = pltpu.get_barrier_semaphore()
    pl.semaphore_signal(barrier, inc=1, device_id=across, device_id_type=MESH)
    for bit in range(bits):
        pl.semaphore_signal(barrier, inc=1, device_id=peer(bit)[1], device_id_type=MESH)
    pl.semaphore_wait(barrier, bits + 1)

    @pl.when(section == 0)
    def _():
        up_across.start()

    loads[0].wait()

    row_of = lax.broadcasted_iota(jnp.int32, (PAD, tokens), 0)
    token_of = lax.broadcasted_iota(jnp.int32, (PAD, tokens), 1)
    valid = jnp.zeros((PAD, tokens), F32)
    pad_rows = lax.broadcasted_iota(jnp.int32, (PAD, 1), 0)
    lengths = jnp.ones((PAD, 1), F32)
    labels = jnp.full((PAD, 1), -1, jnp.int32)
    for m in range(micro):
        seq = lengths_ref[0, m]
        inside = (row_of == m) & (token_of >= m * length) & (token_of < m * length + seq)
        valid = jnp.where(inside, 1.0, valid)
        lengths = jnp.where(pad_rows == m, seq.astype(F32), lengths)
        labels = jnp.where(pad_rows == m, labels_ref[0, m], labels)
    valid = valid.astype(BF16)

    def normalised(rows):
        values = x_ref[rows, :].astype(F32)
        inv_rms = lax.rsqrt(jnp.mean(values * values, axis=-1, keepdims=True) + EPSILON)
        unit = values * inv_rms
        xn = (unit * gain_ref[...]).astype(BF16)
        xn_ref[rows, :] = xn
        pre_act = contract(xn, wd_ref[...], 1, 0)
        sigma = jax.nn.sigmoid(pre_act)
        h_ref[rows, :] = (pre_act * sigma).astype(BF16)
        return inv_rms, unit, sigma * (1.0 + pre_act * (1.0 - sigma))

    @pl.when(section == 0)
    def _():
        loads[1].wait()
        loads[2].wait()

        @pl.loop(0, tokens // chunk)
        def _(index):
            rows = pl.ds(pl.multiple_of(index * chunk, chunk), chunk)
            slope_ref[rows, :] = normalised(rows)[2]

        pool_across.wait_recv()

    @pl.when(section == 1)
    def _():
        totals = contract(valid, x_ref[...], 1, 0)
        pool_ref[...] = (totals / lengths).astype(BF16)
        pool_across.start()

    pooled = pool_ref[...].astype(F32)
    pooled_inv = lax.rsqrt(jnp.mean(pooled * pooled, axis=-1, keepdims=True) + EPSILON)
    pooled_unit = pooled * pooled_inv
    pooled_normed = jnp.where(section == 0, pooled_unit[:, :band], pooled_unit[:, band:])
    loads[3].wait()
    pre_ref[...] = contract(pooled_normed.astype(BF16), cf_ref[...], 1, 0)
    pre_across.start()
    cs_pad_ref[...] = jnp.zeros(cs_pad_ref.shape, BF16)
    cs_pad_ref[:languages, :] = cs_ref[...]

    @pl.when(section == 1)
    def _():
        for slot in (1, 2, 4, 5):
            loads[slot].wait()

        @pl.loop(0, tokens // chunk)
        def _(index):
            rows = pl.ds(pl.multiple_of(index * chunk, chunk), chunk)
            inv_rms, unit, slope = normalised(rows)
            upstream = g_ref[rows, :]
            grad_hidden = contract(upstream, wu_ref[...], 1, 1)
            da = (grad_hidden * slope).astype(BF16)
            da_ref[rows, :] = da
            scaled = contract(da, wd_ref[...], 1, 1) * gain_ref[...]
            tilt = jnp.mean(scaled * unit, axis=-1, keepdims=True)
            g0_ref[rows, :] = (
                upstream.astype(F32) + inv_rms * (scaled - unit * tilt)
            ).astype(BF16)

        fill(0, xn_ref, da_ref)
        fill(1, g_ref, h_ref)
        up_across.wait_recv()
        up_beside.start()

    pre_across.wait_recv()
    pre = pre_ref[...] + pre_in_ref[...]
    sigma = jax.nn.sigmoid(pre)
    hidden = (pre * sigma).astype(BF16)
    logits = contract(hidden, cs_pad_ref[...], 1, 1)
    language = lax.broadcasted_iota(jnp.int32, (PAD, LANES), 1)
    exponent = jnp.where(language < languages, jnp.exp(logits), 0.0)
    probabilities = exponent / jnp.sum(exponent, axis=-1, keepdims=True)
    onehot = jnp.where(language == labels, 1.0, 0.0)
    grad_logits = (probabilities - onehot).astype(BF16)
    grad_hidden = contract(grad_logits, cs_pad_ref[...], 1, 0)
    grad_pre = (grad_hidden * (sigma * (1.0 + pre * (1.0 - sigma)))).astype(BF16)
    gn_ref[...] = contract(grad_pre, cf_ref[...], 1, 1)

    @pl.when(section == 0)
    def _():
        gn_across.start()
        up_across.wait_send()
        h_across.start()
        for target in range(dp):
            gain_cut_ref[target : target + 1, :] = gain_ref[:, target * cut : (target + 1) * cut]

    pack32_ref[...] = jnp.zeros(pack32_ref.shape, F32)
    pack32_ref[0:micro, :band] = pooled_normed[:micro]
    pack32_ref[micro : 2 * micro, :hidden_width] = hidden.astype(F32)[:micro]
    pack32_ref[2 * micro : 3 * micro, :hidden_width] = grad_pre.astype(F32)[:micro]
    pack32_ref[3 * micro : 4 * micro, :LANES] = grad_logits.astype(F32)[:micro]
    ag_ref[0] = pack32_ref[...].astype(BF16)
    ag_copy(0).start()

    @pl.when(section == 1)
    def _():
        for target in range(dp):
            gain_cut_ref[target : target + 1, :] = gain_ref[:, target * cut : (target + 1) * cut]
        gn_across.wait_recv()
        grad_normed = jnp.concatenate([gn_in_ref[...], gn_ref[...]], axis=1)
        tilt = jnp.mean(grad_normed * pooled_unit, axis=-1, keepdims=True)
        grad_pooled = pooled_inv * (grad_normed - pooled_unit * tilt)
        in_use = pad_rows < micro
        reversal = jnp.where(in_use, -REVERSAL * grad_pooled / lengths, 0.0).astype(BF16)
        up_beside.wait_recv()
        up_reversal = contract(reversal, wu_in_ref[...], 1, 1)
        for m in range(micro):
            rows = pl.ds(m * length, length)
            inside = lax.broadcasted_iota(jnp.int32, (length, 1), 0) < lengths_ref[0, m]
            extra = jnp.where(inside, up_reversal[m : m + 1], 0.0)
            p_ref[rows, :] = (contract(g0_ref[rows, :], wu_in_ref[...], 1, 1) + extra).astype(BF16)
            p_copy(m).start()
        advance(0, 0)
        advance(1, 0)
        h_across.wait_recv()
        masked_h = contract(valid, h0_ref[...], 1, 0).astype(BF16)
        fill(2, g0_ref, h0_ref, (reversal, masked_h))

    def ag_step(step):
        ag_copy(step).wait_recv()
        if step + 1 < bits:
            ag_copy(step + 1).start()

    def critic_outputs():
        blocks = ag_ref[...].reshape(dp * PAD, ag_ref.shape[2])
        total = dp * PAD
        from_row = lax.broadcasted_iota(jnp.int32, (total, total), 1)
        to_row = lax.broadcasted_iota(jnp.int32, (total, total), 0)
        early = lax.rem(to_row, PAD) < 2 * micro
        shift = jnp.where(early & (from_row == to_row + 2 * micro), 1.0, 0.0).astype(BF16)
        own = hidden_width // dp
        at = lax.broadcasted_iota(jnp.int32, (blocks.shape[1], LANES), 0)
        lane = lax.broadcasted_iota(jnp.int32, (blocks.shape[1], LANES), 1)
        pick = jnp.where((at == lane + replica * own) & (lane < own), 1.0, 0.0).astype(BF16)
        picked = contract(blocks, pick, 1, 0)
        place = lax.rem(lax.broadcasted_iota(jnp.int32, (total, LANES), 0), PAD)
        moved_pre = contract(shift, picked.astype(BF16), 1, 0)
        moved_pre = jnp.where(place < micro, moved_pre, 0.0).astype(BF16)
        moved_logits = contract(shift, blocks[:, :LANES], 1, 0).astype(BF16)
        hidden_own = jnp.where((place >= micro) & (place < 2 * micro), picked, 0.0).astype(BF16)
        first_ref[...] = contract(moved_pre, blocks[:, :band], 0, 0)[:own]
        second_ref[...] = contract(moved_logits, hidden_own, 0, 0)[:languages, :own]

    def finish_down():
        reduced = jnp.concatenate(
            [rs_take(0, bits - 1)[0], rs_take(1, bits - 1)[0]], axis=1
        )
        gwd_ref[...] = reduced
        start = pl.multiple_of(replica * cut, cut)
        weighted = reduced * wd_ref[pl.ds(start, cut), :].astype(F32)
        row = lax.dot_general(
            jnp.ones((8, rank), F32),
            weighted,
            (((1,), (1,)), ((), ())),
            precision=lax.Precision.HIGHEST,
            preferred_element_type=F32,
        )
        gain_out_ref[...] = row[0:1] / gain_cut_ref[pl.ds(replica, 1), :]

    @pl.when(section == 1)
    def _():
        ag_step(0)
        for step in range(1, bits):
            if step + 1 < bits:
                advance(0, step)
                advance(1, step)
            ag_step(step)
            if step == 1:
                advance(2, 0)
        for step in range(1, bits - 1):
            advance(2, step)
        critic_outputs()
        for side in range(2):
            last_ref[side] = rs_take(4 + side, bits - 1)[0]
            last_across[side].start()
        finish_down()
        for side in range(2):
            gwu_ref[:, side * half_rank : (side + 1) * half_rank] = rs_take(2 + side, bits - 1)[0]

    @pl.when(section == 0)
    def _():
        for step in range(bits):
            ag_step(step)
        critic_outputs()
        for m in range(micro):
            p_copy(m).wait_recv()
            rows = pl.ds(m * length, length)
            da_ref[rows, :] = (p_in_ref[rows, :].astype(F32) * slope_ref[rows, :]).astype(BF16)
        fill(0, xn_ref, da_ref)
        for step in range(bits - 1):
            advance(0, step)
        finish_down()
        for side in range(2):
            last_across[side].wait_recv()
            gwu_ref[:, side * half_rank : (side + 1) * half_rank] = last_in_ref[side]

    pre_across.wait_send()
    for step in range(bits):
        ag_copy(step).wait_send()
        rs_copy(0, step).wait_send()
        rs_copy(1, step).wait_send()

    @pl.when(section == 0)
    def _():
        h_across.wait_send()
        gn_across.wait_send()

    @pl.when(section == 1)
    def _():
        up_beside.wait_send()
        pool_across.wait_send()
        for m in range(micro):
            p_copy(m).wait_send()
        for side in range(2):
            last_across[side].wait_send()
        for step in range(bits):
            for job in range(2, 6):
                rs_copy(job, step).wait_send()


def hand_over(*refs):
    sems = refs[-1]
    count = (len(refs) - 1) // 2
    copies = [
        pltpu.make_async_copy(refs[slot], refs[count + slot], sems.at[slot])
        for slot in range(count)
    ]
    for copy in copies:
        copy.start()
    for copy in copies:
        copy.wait()


def fused_body(
    section_in,
    top_grad,
    seq_lengths,
    lang_labels,
    norm_gain,
    w_down,
    w_up,
    critic_first,
    critic_second,
):
    dp = lax.axis_size("dp")
    bits = dp.bit_length() - 1
    micro, _, length, features = section_in.shape[1:]
    tokens = micro * length
    rank = w_down.shape[2]
    band, hidden_width = critic_first.shape
    languages = critic_second.shape[1]
    cut = features // dp
    width = max(band, hidden_width)
    chunk = min(2 * length, tokens)
    jobs = []
    for _ in range(6):
        jobs += [pltpu.VMEM((dp >> step, cut, rank // 2), BF16) for step in range(bits)]
        jobs += [pltpu.VMEM((dp >> (step + 1), cut, rank // 2), BF16) for step in range(bits)]
    vmem = pl.BlockSpec(memory_space=pltpu.VMEM)
    smem = pl.BlockSpec(memory_space=pltpu.SMEM)
    anywhere = pl.BlockSpec(memory_space=pl.ANY)
    results = (
        jax.ShapeDtypeStruct((cut, rank), F32),
        jax.ShapeDtypeStruct((cut, rank), F32),
        jax.ShapeDtypeStruct((1, cut), F32),
        jax.ShapeDtypeStruct((hidden_width // dp, band), F32),
        jax.ShapeDtypeStruct((languages, hidden_width // dp), F32),
    )
    held = pl.pallas_call(
        functools.partial(relay_kernel, (micro, length, bits, chunk)),
        out_shape=results,
        in_specs=[smem, smem] + [anywhere] * 6 + [vmem],
        out_specs=(vmem,) * 5,
        scratch_shapes=[
            pltpu.VMEM((tokens, features), BF16),
            pltpu.VMEM((tokens, features), BF16),
            pltpu.VMEM((1, features), F32),
            pltpu.VMEM((features, rank), BF16),
            pltpu.VMEM((rank, features), BF16),
            pltpu.VMEM((band, hidden_width), BF16),
            pltpu.VMEM((dp, cut), F32),
            pltpu.VMEM((tokens, features), BF16),
            pltpu.VMEM((tokens, features), BF16),
            pltpu.VMEM((tokens, rank), BF16),
            pltpu.VMEM((tokens, rank), BF16),
            pltpu.VMEM((tokens, rank), F32),
            pltpu.VMEM((rank, features), BF16),
            pltpu.VMEM((tokens, rank), BF16),
            pltpu.VMEM((tokens, rank), BF16),
            pltpu.VMEM((tokens, rank), BF16),
            pltpu.VMEM((PAD, features), BF16),
            pltpu.VMEM((PAD, hidden_width), F32),
            pltpu.VMEM((PAD, hidden_width), F32),
            pltpu.VMEM((PAD, band), F32),
            pltpu.VMEM((PAD, band), F32),
            pltpu.VMEM((LANES, hidden_width), BF16),
            pltpu.VMEM((PAD, width), F32),
            pltpu.VMEM((dp, PAD, width), BF16),
            pltpu.VMEM((2, cut, rank // 2), F32),
            pltpu.VMEM((2, cut, rank // 2), F32),
            *jobs,
            pltpu.SemaphoreType.DMA((6,)),
            pltpu.SemaphoreType.DMA((16,)),
            pltpu.SemaphoreType.DMA((2 * micro,)),
            pltpu.SemaphoreType.DMA((2 * bits,)),
            pltpu.SemaphoreType.DMA((12 * bits,)),
        ],
        compiler_params=pltpu.CompilerParams(
            collective_id=0, has_side_effects=True, vmem_limit_bytes=58 * 2**20
        ),
        cost_estimate=pl.CostEstimate(
            flops=12 * tokens * features * rank, bytes_accessed=8 * 2**20, transcendentals=0
        ),
    )(
        seq_lengths.T,
        lang_labels.T,
        section_in.reshape(tokens, features),
        top_grad.reshape(tokens, features),
        norm_gain,
        w_down[0],
        w_up[0],
        critic_first,
        critic_second.T,
    )
    gwd, gwu, gain, first, second = pl.pallas_call(
        hand_over,
        out_shape=results,
        in_specs=[anywhere] * 5,
        out_specs=(anywhere,) * 5,
        scratch_shapes=[pltpu.SemaphoreType.DMA((5,))],
    )(*held)
    return (gwd[None], gwu.T[None], gain, first.T, second.T)


def from_root(array, axis, root):
    mine = lax.axis_index(axis) == root
    return lax.psum(jnp.where(mine, array, jnp.zeros_like(array)), axis)


def from_behind(block, axis, distance):
    devices = range(lax.axis_size(axis))
    route = [(i - distance, i) for i in devices if i - distance in devices]
    return lax.ppermute(block, axis, route)


def silu_slope(pre_act):
    sigma = jax.nn.sigmoid(pre_act)
    return sigma * (1.0 + pre_act * (1.0 - sigma))


def inner_rows(left, right):
    return lax.dot_general(
        left, right, (((0,), (0,)), ((), ())), preferred_element_type=jnp.float32
    )


def adapter_backward(local_rows, upstream, gain_row, down_proj, up_proj):
    values = local_rows.astype(jnp.float32)
    inv_rms = lax.rsqrt(jnp.mean(values * values, axis=-1, keepdims=True) + EPSILON)
    unit_rows = values * inv_rms
    normed = (unit_rows * gain_row[None, :]).astype(jnp.bfloat16)
    pre_act = jnp.dot(normed, down_proj, preferred_element_type=jnp.float32)
    hidden = jax.nn.silu(pre_act).astype(jnp.bfloat16)
    grad_up = inner_rows(hidden, upstream)
    grad_hidden = jnp.dot(upstream, up_proj.T, preferred_element_type=jnp.float32)
    grad_pre = (grad_hidden * silu_slope(pre_act)).astype(jnp.bfloat16)
    grad_down = inner_rows(normed, grad_pre)
    grad_normed = jnp.dot(grad_pre, down_proj.T, preferred_element_type=jnp.float32)
    grad_gain = jnp.sum(grad_normed * unit_rows, axis=0)
    scaled = grad_normed * gain_row[None, :]
    grad_input = upstream.astype(jnp.float32) + inv_rms * (
        scaled - unit_rows * jnp.mean(scaled * unit_rows, axis=-1, keepdims=True)
    )
    return (grad_input, grad_down, grad_up, grad_gain)


def critic_pass(pooled, lang_labels, critic_first, critic_second, section_place):
    batch_rows = pooled.shape[0] * pooled.shape[1]
    features = pooled.shape[2]
    values = pooled.reshape(batch_rows, features).astype(jnp.float32)
    inv_rms = lax.rsqrt(jnp.mean(values * values, axis=-1, keepdims=True) + EPSILON)
    unit_rows = values * inv_rms
    normed = unit_rows.astype(jnp.bfloat16)
    band_rows = critic_first.shape[0]
    normed_band = lax.dynamic_slice_in_dim(normed, section_place * band_rows, band_rows, 1)
    full_first = lax.all_gather(critic_first, "section", axis=0, tiled=True)
    pre_act = jnp.dot(normed, full_first, preferred_element_type=jnp.float32)
    hidden = jax.nn.silu(pre_act).astype(jnp.bfloat16)
    logits = jnp.dot(hidden, critic_second, preferred_element_type=jnp.float32)
    exponent = jnp.exp(logits)
    probabilities = exponent / jnp.sum(exponent, axis=-1, keepdims=True)
    onehot = (
        lang_labels.reshape(batch_rows)[:, None] == jnp.arange(critic_second.shape[1])[None, :]
    ).astype(jnp.float32)
    grad_logits = (probabilities - onehot).astype(jnp.bfloat16)
    grad_second = inner_rows(hidden, grad_logits)
    grad_hidden = jnp.dot(grad_logits, critic_second.T, preferred_element_type=jnp.float32)
    grad_pre = (grad_hidden * silu_slope(pre_act)).astype(jnp.bfloat16)
    grad_first = inner_rows(normed_band, grad_pre)
    grad_normed = jnp.dot(grad_pre, full_first.T, preferred_element_type=jnp.float32)
    grad_pooled = inv_rms * (
        grad_normed - unit_rows * jnp.mean(grad_normed * unit_rows, axis=-1, keepdims=True)
    )
    return (grad_first, grad_second, grad_pooled)


def body(
    section_in,
    top_grad,
    seq_lengths,
    lang_labels,
    norm_gain,
    w_down,
    w_up,
    critic_first,
    critic_second,
):
    sections = lax.axis_size("section")
    section_place = lax.axis_index("section")
    target = sections // 2
    inputs = section_in[0]
    gain_row = norm_gain[0]
    down_proj = w_down[0]
    up_proj = w_up[0]
    micro_count, seq_dev, seq_len, features = inputs.shape
    token_rows = seq_dev * seq_len
    positions = jnp.arange(seq_len)
    valid_mask = positions[None, None, :] < seq_lengths[:, :, None]
    mask_values = valid_mask.astype(jnp.float32)
    lengths = seq_lengths.astype(jnp.float32)
    totals = jnp.einsum(
        "mnt,mntd->mnd", valid_mask.astype(jnp.bfloat16), inputs, preferred_element_type=jnp.float32
    )
    pooled = (totals / lengths[:, :, None]).astype(jnp.bfloat16)
    pooled = from_root(pooled, "section", target)
    grad_first, grad_second, grad_pooled = critic_pass(
        pooled, lang_labels, critic_first, critic_second, section_place
    )
    is_target = (section_place == target).astype(jnp.float32)
    reversal = (
        -REVERSAL
        * is_target
        * grad_pooled.reshape(micro_count, seq_dev, features)
        / lengths[:, :, None]
    )
    is_last = section_place == sections - 1

    def advance(moment, carry):
        incoming, down_sum, up_sum, gain_sum = carry
        micro_now = moment - (sections - 1 - section_place)
        is_live = (micro_now >= 0) & (micro_now < micro_count)
        slot_index = jnp.clip(micro_now, 0, micro_count - 1)
        local_rows = lax.dynamic_index_in_dim(inputs, slot_index, 0, keepdims=False).reshape(
            token_rows, features
        )
        top_rows = lax.dynamic_index_in_dim(top_grad, slot_index, 0, keepdims=False).reshape(
            token_rows, features
        )
        upstream = jnp.where(is_last, top_rows, incoming)
        reverse_rows = lax.dynamic_index_in_dim(reversal, slot_index, 0, keepdims=False)
        mask_rows = lax.dynamic_index_in_dim(mask_values, slot_index, 0, keepdims=False)
        extra = (reverse_rows[:, None, :] * mask_rows[:, :, None]).reshape(token_rows, features)

        def active(operand):
            grad_input, grad_down, grad_up, grad_gain = adapter_backward(
                local_rows, upstream, gain_row, down_proj, up_proj
            )
            return ((grad_input + extra).astype(jnp.bfloat16), grad_down, grad_up, grad_gain)

        def resting(operand):
            return (
                jnp.zeros_like(incoming),
                jnp.zeros_like(down_sum),
                jnp.zeros_like(up_sum),
                jnp.zeros_like(gain_sum),
            )

        outgoing, grad_down, grad_up, grad_gain = lax.cond(is_live, active, resting, 0)
        received = from_behind(outgoing, "section", -1)
        return (received, down_sum + grad_down, up_sum + grad_up, gain_sum + grad_gain)

    initial = (
        jnp.zeros((token_rows, features), jnp.bfloat16),
        jnp.zeros(down_proj.shape, jnp.float32),
        jnp.zeros(up_proj.shape, jnp.float32),
        jnp.zeros((features,), jnp.float32),
    )
    finished = lax.fori_loop(0, micro_count + sections - 1, advance, initial)
    summed = (
        lax.psum_scatter(finished[1], "dp", scatter_dimension=0, tiled=True),
        lax.psum_scatter(finished[2], "dp", scatter_dimension=1, tiled=True),
        lax.psum_scatter(finished[3], "dp", scatter_dimension=0, tiled=True),
        lax.psum_scatter(grad_first, "dp", scatter_dimension=1, tiled=True),
        lax.psum_scatter(grad_second, "dp", scatter_dimension=0, tiled=True),
    )
    return (summed[0][None], summed[1][None], summed[2][None], summed[3], summed[4])


def solution(mesh):
    sections, replicas = mesh.shape["section"], mesh.shape["dp"]

    def program(*args):
        micro, sequences = args[2].shape
        fits = (
            sections == 2
            and sequences == replicas
            and replicas >= 4
            and replicas & (replicas - 1) == 0
            and micro * 4 == PAD
            and args[4].shape[1] % (replicas * 2 * PAD) == 0
            and args[5].shape[2] % (2 * LANES) == 0
        )
        return placed(mesh, fused_body if fits else body)(*args)

    return program


def placed(mesh, device_body):
    return jax.shard_map(
        device_body,
        mesh=mesh,
        in_specs=(
            P("section", None, "dp", None, None),
            P(None, "dp", None, None),
            P(None, "dp"),
            P(None, "dp"),
            P("section", None),
            P("section", None, None),
            P("section", None, None),
            P("section", None),
            P(),
        ),
        out_specs=(
            P("section", "dp", None),
            P("section", None, "dp"),
            P("section", "dp"),
            P("section", "dp"),
            P("dp", None),
        ),
        check_vma=False,
    )
```
